256 devices in a mesh: section: 32 (over y_hi, z, core), tp: 8 (over y_lo, x).
Axes of the slice: x: 4, y: 4 (y_hi: 2, y_lo: 2; y = y_hi * 2 + y_lo), z: 8, core: 2. Of those that a mesh axis runs over, the one named last changes fastest.
Arguments:
- query_key_value_weight: bfloat16 [32, 2048, 3, 2048], P('section', None, None, 'tp'), may hold values from -6 to 6
- output_weight: bfloat16 [32, 2048, 2048], P('section', 'tp'), may hold values from -0.125 to 0.125
- ascending_query_key_value_weight: bfloat16 [32, 2048, 3, 2048], P('section', None, None, 'tp'), may hold values from -6 to 6
- ascending_output_weight: bfloat16 [32, 2048, 2048], P('section', 'tp'), may hold values from -0.125 to 0.125
- descending_saved_input: bfloat16 [32, 3, 128, 2048], P('section', None, 'tp'), may hold values from -6 to 6
- ascending_saved_input: bfloat16 [32, 3, 128, 2048], P('section', None, 'tp'), may hold values from -6 to 6
- descending_transit_gradient: bfloat16 [32, 128, 2048], P('section', 'tp'), may hold values from -4 to 4
- ascending_transit_gradient: bfloat16 [32, 128, 2048], P('section', 'tp'), may hold values from -4 to 4
- descending_loss_gradient: bfloat16 [2, 128, 2048], P(None, 'tp'), may hold values from -4 to 4
- ascending_loss_gradient: bfloat16 [2, 128, 2048], P(None, 'tp'), may hold values from -4 to 4
Outputs:
- grad_qkv: bfloat16 [32, 2048, 3, 2048], P('section', None, None, 'tp')
- grad_out: bfloat16 [32, 2048, 2048], P('section', 'tp')
- final_down: bfloat16 [32, 128, 2048], P('section', 'tp')
- final_up: bfloat16 [32, 128, 2048], P('section', 'tp')
The draws below stay inside these ranges and needn't reach their ends.
All inputs are finite; a program needn't handle non-finite values.
Results may differ from the reference program's by a relative error of at most 0.029.
Values may be sent and summed in bfloat16 or wider, within the bound.
No kernel may reach another device: no remote copies, remote signals or barrier semaphores. Data moves between devices by JAX's collectives and lax.ppermute only.
A program may use at most 128 MiB of HBM per device.

```python
import jax
import jax.numpy as jnp
from jax import lax

MODEL_WIDTH = 2048
HEADS = 16
HEAD = 128
MICRO_TOKENS = 128
TICKS = 3
HD = 2048
LAYER_COUNT = 32


def drawn_qkv(normal_key):
    return jnp.clip(jax.random.normal(normal_key, (LAYER_COUNT, MODEL_WIDTH, 3, HD), jnp.float32), -6.0, 6.0) * MODEL_WIDTH ** (-0.5)


def draw_query_key_value_weight(key, part):
    key = jax.random.fold_in(key, 7)
    normal_key = jax.random.fold_in(key, 0)
    drawn = drawn_qkv(normal_key)
    return drawn.astype(jnp.bfloat16)


def draw_ascending_query_key_value_weight(key, part):
    key = jax.random.fold_in(key, 11)
    normal_key = jax.random.fold_in(key, 0)
    drawn = drawn_qkv(normal_key)
    return drawn.astype(jnp.bfloat16)


def block_scale(stream_key, dims, cuts, least, top_value):
    level = 1.0
    for position, shards_of in cuts:
        heights = jax.random.uniform(jax.random.fold_in(jax.random.fold_in(stream_key, 6), position), (shards_of,), jnp.float32, least / len(cuts), top_value / len(cuts))
        level = level * jnp.repeat(jnp.exp(heights), dims[position] // shards_of).reshape((-1,) + (1,) * (len(dims) - 1 - position))
    return level


def centred(rng, shape, scale, most, shards=(), dtype=jnp.bfloat16):
    values = jax.random.normal(rng, shape, jnp.float32) * scale
    if len(shards) > 0:
        values = block_scale(rng, shape, shards, -0.22, 0.18) * values
    return jnp.clip(values, min=-most, max=most).astype(dtype)


def setup_inputs(seed: int = 0) -> dict:
    key_of = jax.random.split(jax.random.key(seed), 11)
    return {
        "query_key_value_weight": draw_query_key_value_weight(jax.random.fold_in(key_of[10], 71), 0),
        "output_weight": centred(key_of[1], (LAYER_COUNT, HD, MODEL_WIDTH), HD ** -0.5, 0.125, ((0, 32), (1, 8))),
        "ascending_query_key_value_weight": draw_ascending_query_key_value_weight(jax.random.fold_in(key_of[10], 71), 0),
        "ascending_output_weight": centred(key_of[3], (LAYER_COUNT, HD, MODEL_WIDTH), HD ** -0.5, 0.125, ((0, 32), (1, 8))),
        "descending_saved_input": centred(key_of[4], (LAYER_COUNT, TICKS, MICRO_TOKENS, MODEL_WIDTH), 1.0, 6.0, ((0, 32), (2, 8))),
        "ascending_saved_input": centred(key_of[5], (LAYER_COUNT, TICKS, MICRO_TOKENS, MODEL_WIDTH), 1.0, 6.0, ((0, 32), (2, 8))),
        "descending_transit_gradient": centred(key_of[6], (LAYER_COUNT, MICRO_TOKENS, MODEL_WIDTH), 0.3, 4.0, ((0, 32), (1, 8))),
        "ascending_transit_gradient": centred(key_of[7], (LAYER_COUNT, MICRO_TOKENS, MODEL_WIDTH), 0.3, 4.0, ((0, 32), (1, 8))),
        "descending_loss_gradient": centred(key_of[8], (TICKS - 1, MICRO_TOKENS, MODEL_WIDTH), 0.3, 4.0, ((1, 8),)),
        "ascending_loss_gradient": centred(key_of[9], (TICKS - 1, MICRO_TOKENS, MODEL_WIDTH), 0.3, 4.0, ((1, 8),)),
    }


EPSILON = 1e-05

def layer_step(weights_qkv, weights_out, stored, upstream):
    score_scale = HEAD ** (-0.5)
    raw = stored.astype(jnp.float32)
    centre = raw - lax.optimization_barrier(jnp.mean(raw, axis=-1, keepdims=True))
    inverse = lax.rsqrt(lax.optimization_barrier(jnp.mean(centre * centre, axis=-1, keepdims=True)) + EPSILON)
    normed = centre * inverse
    hidden = normed.astype(jnp.bfloat16)
    flat_qkv = weights_qkv.reshape(MODEL_WIDTH, 3 * HD)
    project = jnp.dot(hidden, flat_qkv, preferred_element_type=jnp.float32).astype(jnp.bfloat16)
    project = project.reshape(MICRO_TOKENS, 3, HEADS, HEAD)
    queries = project[:, 0].astype(jnp.float32)
    key_rows = project[:, 1].astype(jnp.float32)
    value_rows = project[:, 2].astype(jnp.float32)
    scores = jnp.einsum('qhe,khe->hqk', queries, key_rows, precision=lax.Precision.HIGHEST) * score_scale
    causal = lax.broadcasted_iota(jnp.int32, (MICRO_TOKENS, MICRO_TOKENS), 0) >= lax.broadcasted_iota(jnp.int32, (MICRO_TOKENS, MICRO_TOKENS), 1)
    weights_soft = jax.nn.softmax(jnp.where(causal, scores, -jnp.inf), axis=-1)
    soft_half = weights_soft.astype(jnp.bfloat16).astype(jnp.float32)
    attended = jnp.einsum('hqk,khe->qhe', soft_half, value_rows, precision=lax.Precision.HIGHEST).astype(jnp.bfloat16)
    grad_out = jnp.dot(attended.reshape(MICRO_TOKENS, HD).T, upstream, preferred_element_type=jnp.float32)
    d_attended = jnp.dot(upstream, weights_out.T, preferred_element_type=jnp.float32).astype(jnp.bfloat16)
    d_attended = d_attended.reshape(MICRO_TOKENS, HEADS, HEAD).astype(jnp.float32)
    d_values = jnp.einsum('hqk,qhe->khe', soft_half, d_attended, precision=lax.Precision.HIGHEST).astype(jnp.bfloat16)
    d_probs = jnp.einsum('qhe,khe->hqk', d_attended, value_rows, precision=lax.Precision.HIGHEST)
    offset = jnp.einsum('qhe,qhe->hq', d_attended, attended.astype(jnp.float32), precision=lax.Precision.HIGHEST)
    d_scores = (weights_soft * (d_probs - offset[:, :, None]) * score_scale).astype(jnp.bfloat16).astype(jnp.float32)
    d_queries = jnp.einsum('hqk,khe->qhe', d_scores, key_rows, precision=lax.Precision.HIGHEST).astype(jnp.bfloat16)
    d_keys = jnp.einsum('hqk,qhe->khe', d_scores, queries, precision=lax.Precision.HIGHEST).astype(jnp.bfloat16)
    d_project = jnp.stack([d_queries, d_keys, d_values], axis=1).reshape(MICRO_TOKENS, 3 * HD)
    grad_qkv = jnp.dot(hidden.T, d_project, preferred_element_type=jnp.float32).reshape(MODEL_WIDTH, 3, HD)
    d_hidden = jnp.dot(d_project, flat_qkv.T, preferred_element_type=jnp.float32)
    backward = inverse * (d_hidden - lax.optimization_barrier(jnp.mean(d_hidden, axis=-1, keepdims=True)) - normed * lax.optimization_barrier(jnp.mean(d_hidden * normed, axis=-1, keepdims=True)))
    departing_gradient = (upstream.astype(jnp.float32) + backward).astype(jnp.bfloat16)
    return (departing_gradient, grad_qkv, grad_out)

def execute_relay_backward(query_key_value_weight, output_weight, saved_layer_input, transit_gradient, loss_gradient):
    arriving_gradient = transit_gradient
    sum_qkv = jnp.zeros((LAYER_COUNT, MODEL_WIDTH, 3, HD), jnp.float32)
    sum_out = jnp.zeros((LAYER_COUNT, HD, MODEL_WIDTH), jnp.float32)
    departing_gradient = transit_gradient
    for tick_index in range(TICKS):

        def one_layer(packed):
            weights_qkv, weights_out, stored, upstream, total_qkv, total_out = packed
            result, piece_qkv, piece_out = layer_step(weights_qkv, weights_out, stored, upstream)
            return (result, total_qkv + piece_qkv, total_out + piece_out)
        departing_gradient, sum_qkv, sum_out = lax.map(one_layer, (query_key_value_weight, output_weight, saved_layer_input[:, tick_index], arriving_gradient, sum_qkv, sum_out))
        if tick_index + 1 < TICKS:
            arriving_gradient = jnp.concatenate([departing_gradient[1:], loss_gradient[tick_index][None]], axis=0)
    return (departing_gradient, sum_qkv.astype(jnp.bfloat16), sum_out.astype(jnp.bfloat16))

def reference(query_key_value_weight, output_weight, ascending_query_key_value_weight, ascending_output_weight, descending_saved_input, ascending_saved_input, descending_transit_gradient, ascending_transit_gradient, descending_loss_gradient, ascending_loss_gradient):
    descending_final_layer, descending_query_key_value, descending_output_gradient = execute_relay_backward(query_key_value_weight, output_weight, descending_saved_input, descending_transit_gradient, descending_loss_gradient)
    ascending_final_section, ascending_query_key_value, ascending_output_gradient = execute_relay_backward(ascending_query_key_value_weight[::-1], ascending_output_weight[::-1], ascending_saved_input[::-1], ascending_transit_gradient[::-1], ascending_loss_gradient)
    grad_qkv = (descending_query_key_value.astype(jnp.float32) + ascending_query_key_value.astype(jnp.float32)).astype(jnp.bfloat16)
    grad_out = (descending_output_gradient.astype(jnp.float32) + ascending_output_gradient.astype(jnp.float32)).astype(jnp.bfloat16)
    return (grad_qkv, grad_out, descending_final_layer, ascending_final_section[::-1])
```

```python
import functools

import jax
import jax.numpy as jnp
from jax import lax
from jax.experimental import pallas as pl
from jax.experimental.pallas import tpu as pltpu
from jax.sharding import PartitionSpec as P

HEAD = 128
TICKS = 3
EPSILON = 1e-05
MIB = 1 << 20
VMEM = pl.BlockSpec(memory_space=pltpu.VMEM)


def dot_nn(left, right):
    return jnp.dot(left, right, preferred_element_type=jnp.float32)


def dot_nt(left, right):
    return lax.dot_general(left, right, (((1,), (1,)), ((), ())), preferred_element_type=jnp.float32)


def dot_tn(left, right):
    return lax.dot_general(left, right, (((0,), (0,)), ((), ())), preferred_element_type=jnp.float32)


def normalized(raw):
    centre = raw - jnp.mean(raw, axis=-1, keepdims=True)
    inverse = lax.rsqrt(jnp.mean(centre * centre, axis=-1, keepdims=True) + EPSILON)
    return centre * inverse, inverse


def local_call(body, out_shape, operands, flops, moved, limit=16 * MIB):
    return pl.pallas_call(
        body,
        out_shape=out_shape,
        in_specs=[VMEM] * len(operands),
        out_specs=jax.tree.map(lambda _: VMEM, out_shape),
        compiler_params=pltpu.CompilerParams(vmem_limit_bytes=limit),
        cost_estimate=pl.CostEstimate(flops=flops, bytes_accessed=moved, transcendentals=0),
    )(*operands)


def normalize_body(down_ref, up_ref, first_ref, later_ref, up_out_ref):
    down = normalized(down_ref[...].astype(jnp.float32))[0].astype(jnp.bfloat16)
    up = normalized(up_ref[...].astype(jnp.float32))[0].astype(jnp.bfloat16)
    first_ref[0] = down[0]
    first_ref[1] = up[0]
    later_ref[0] = down[1]
    later_ref[1] = down[2]
    later_ref[2] = up[1]
    later_ref[3] = up[2]
    up_out_ref[...] = up


def forward_body(picks, h_ref, w_ref, *outs):
    count = len(picks)
    rows = h_ref.shape[0] * h_ref.shape[2]
    features = h_ref.shape[3]
    local = w_ref.shape[2]
    blocks = [h_ref[:, pick].reshape(rows, features) for pick in picks]
    hidden = blocks[0] if count == 1 else jnp.concatenate(blocks, axis=0)
    queries, keys, values = [dot_nn(hidden, w_ref[part]).astype(jnp.bfloat16) for part in range(3)]
    causal = lax.broadcasted_iota(jnp.int32, (rows, rows), 0) >= lax.broadcasted_iota(
        jnp.int32, (rows, rows), 1
    )
    for index in range(count):
        qkv_ref, soft_ref, a_ref = outs[3 * index : 3 * index + 3]
        span = slice(index * rows, (index + 1) * rows)
        for part, full in enumerate((queries, keys, values)):
            qkv_ref[part] = full[span]
        for head in range(local // HEAD):
            cols = slice(head * HEAD, (head + 1) * HEAD)
            scores = dot_nt(queries[span, cols], keys[span, cols]) * HEAD ** (-0.5)
            scores = jnp.where(causal, scores, -jnp.inf)
            powers = jnp.exp(scores - jnp.max(scores, axis=-1, keepdims=True))
            soft = powers / jnp.sum(powers, axis=-1, keepdims=True)
            soft_ref[head] = soft
            a_ref[:, cols] = dot_nn(soft.astype(jnp.bfloat16), values[span, cols]).astype(
                jnp.bfloat16
            )


def forward(hidden, picks, weights):
    rows = hidden.shape[0] * hidden.shape[2]
    features, local = weights.shape[1:]
    heads = local // HEAD
    one = [
        jax.ShapeDtypeStruct((3, rows, local), jnp.bfloat16),
        jax.ShapeDtypeStruct((heads, rows, rows), jnp.float32),
        jax.ShapeDtypeStruct((rows, local), jnp.bfloat16),
    ]
    count = len(picks)
    outs = local_call(
        functools.partial(forward_body, picks),
        one * count,
        (hidden, weights),
        flops=2 * count * rows * features * 3 * local,
        moved=4 * MIB,
    )
    return [outs[3 * index : 3 * index + 3] for index in range(count)]


def backward_body(g_ref, qkv_ref, soft_ref, a_ref, w_ref, o_ref, part_ref, factor_ref):
    shards, shard_rows, features = g_ref.shape
    rows = shards * shard_rows
    local = o_ref.shape[0]
    upstream = g_ref[...].reshape(rows, features)
    d_attended = dot_nt(upstream, o_ref[...]).astype(jnp.bfloat16)
    d_queries, d_keys, d_values = [], [], []
    for head in range(local // HEAD):
        cols = slice(head * HEAD, (head + 1) * HEAD)
        queries, keys, values = [qkv_ref[part, :, cols] for part in range(3)]
        soft = soft_ref[head]
        d_here = d_attended[:, cols]
        d_values.append(dot_tn(soft.astype(jnp.bfloat16), d_here).astype(jnp.bfloat16))
        d_probs = dot_nt(d_here, values)
        offset = jnp.sum(
            d_here.astype(jnp.float32) * a_ref[:, cols].astype(jnp.float32), axis=-1, keepdims=True
        )
        d_scores = (soft * (d_probs - offset) * HEAD ** (-0.5)).astype(jnp.bfloat16)
        d_queries.append(dot_nn(d_scores, keys).astype(jnp.bfloat16))
        d_keys.append(dot_tn(d_scores, queries).astype(jnp.bfloat16))
    pieces = [jnp.concatenate(parts, axis=1) for parts in (d_queries, d_keys, d_values)]
    for part in range(3):
        factor_ref[part] = pieces[part]
    factor_ref[3] = a_ref[...]
    tile = 512
    for start in range(0, features, tile):
        total = dot_nt(pieces[0], w_ref[0, start : start + tile, :])
        total += dot_nt(pieces[1], w_ref[1, start : start + tile, :])
        total += dot_nt(pieces[2], w_ref[2, start : start + tile, :])
        part_ref[:, :, start : start + tile] = total.astype(jnp.bfloat16).reshape(
            shards, shard_rows, tile
        )


def backward(gathered, saved, weights, weights_out):
    shards, shard_rows, features = gathered.shape
    rows = shards * shard_rows
    local = weights_out.shape[0]
    return local_call(
        backward_body,
        [
            jax.ShapeDtypeStruct((shards, shard_rows, features), jnp.bfloat16),
            jax.ShapeDtypeStruct((4, rows, local), jnp.bfloat16),
        ],
        (gathered, *saved, weights, weights_out),
        flops=2 * rows * features * 4 * local,
        moved=6 * MIB,
    )


def layer_back_body(other_end, parts_ref, x_ref, g_ref, loss_ref, y_ref):
    summed = jnp.sum(parts_ref[...].astype(jnp.float32), axis=0)
    normed, inverse = normalized(x_ref[...].astype(jnp.float32))
    backward = inverse * (
        summed
        - jnp.mean(summed, axis=-1, keepdims=True)
        - normed * jnp.mean(summed * normed, axis=-1, keepdims=True)
    )
    result = (g_ref[...].astype(jnp.float32) + backward).astype(jnp.bfloat16)
    if other_end is not None:
        result = jnp.where(lax.axis_index("section") == other_end, loss_ref[...], result)
    y_ref[...] = result


def layer_back(parts, stored, upstream, loss, other_end):
    return local_call(
        functools.partial(layer_back_body, other_end),
        jax.ShapeDtypeStruct(upstream.shape, jnp.bfloat16),
        (parts, stored, upstream, loss),
        flops=20 * parts.size,
        moved=2 * parts.size,
    )


def gradients_body(h0, later, mirrored, g0, g1, g2, n1, n2, *rest):
    factors, (w_ref, o_ref, d_all, a_all) = rest[:6], rest[6:]
    rows = factors[0].shape[1]

    @pl.when(pl.program_id(0) == 0)
    def _():
        for index, factor in enumerate(factors):
            for part in range(3):
                d_all[part, index * rows : (index + 1) * rows, :] = factor[part]
            a_all[:, index * rows : (index + 1) * rows] = factor[3].T

    tile = h0.shape[-1]

    def flat(block):
        return block.reshape(rows, tile)

    hidden = jnp.concatenate(
        [flat(h0[:, 0]), flat(later[:, 0]), flat(later[:, 1])]
        + [flat(mirrored[:, index]) for index in range(3)],
        axis=0,
    )
    upstream = jnp.concatenate(
        [flat(g0[...]), flat(g1[...]), flat(g2[...]), flat(mirrored[:, 3]), flat(n1[...]), flat(n2[...])],
        axis=0,
    )
    turned = hidden.T
    for part in range(3):
        w_ref[part] = dot_nn(turned, d_all[part]).astype(jnp.bfloat16)
    o_ref[...] = dot_nn(a_all[...], upstream).astype(jnp.bfloat16)


def gradients(first, later, mirrored, flows, mirrored_flows, factors, mirrored_factors):
    features = first.shape[-1]
    rows, local = factors[0].shape[1:]
    tile = 256
    shards = first.shape[0]
    shard_rows = first.shape[2]

    def four(count):
        return pl.BlockSpec((shards, count, shard_rows, tile), lambda i: (0, 0, 0, i))

    three = pl.BlockSpec((shards, shard_rows, tile), lambda i: (0, 0, i))
    whole = pl.BlockSpec((4, rows, local), lambda i: (0, 0, 0))
    depth = 6 * rows
    return pl.pallas_call(
        gradients_body,
        grid=(features // tile,),
        out_shape=[
            jax.ShapeDtypeStruct((3, features, local), jnp.bfloat16),
            jax.ShapeDtypeStruct((local, features), jnp.bfloat16),
        ],
        in_specs=[four(1), four(2), four(4)] + [three] * 5 + [whole] * 6,
        out_specs=[
            pl.BlockSpec((3, tile, local), lambda i: (0, i, 0)),
            pl.BlockSpec((local, tile), lambda i: (0, i)),
        ],
        scratch_shapes=[
            pltpu.VMEM((3, depth, local), jnp.bfloat16),
            pltpu.VMEM((local, depth), jnp.bfloat16),
        ],
        compiler_params=pltpu.CompilerParams(vmem_limit_bytes=24 * MIB),
        cost_estimate=pl.CostEstimate(
            flops=2 * depth * features * 4 * local, bytes_accessed=12 * MIB, transcendentals=0
        ),
    )(first, later, mirrored, *flows, *mirrored_flows, *factors, *mirrored_factors)


def spread(rows):
    count = lax.axis_size("tp")
    return lax.all_to_all(
        jnp.broadcast_to(rows[None], (count,) + rows.shape), "tp", split_axis=0, concat_axis=0, tiled=True
    )


def exchanged(parts):
    return lax.all_to_all(parts, "tp", split_axis=0, concat_axis=0, tiled=True)


def per_device(
    query_key_value_weight,
    output_weight,
    ascending_query_key_value_weight,
    ascending_output_weight,
    descending_saved_input,
    ascending_saved_input,
    descending_transit_gradient,
    ascending_transit_gradient,
    descending_loss_gradient,
    ascending_loss_gradient,
):
    sections = lax.axis_size("section")
    last = sections - 1
    w_down = jnp.transpose(query_key_value_weight[0], (1, 0, 2))
    w_up = jnp.transpose(ascending_query_key_value_weight[0], (1, 0, 2))
    o_down = output_weight[0]
    o_up = ascending_output_weight[0]
    x_down = descending_saved_input[0]
    x_up = ascending_saved_input[0]
    flow_down = descending_transit_gradient[0]
    flow_up = ascending_transit_gradient[0]
    shard_rows, features = flow_up.shape

    lower = [(index, (index - 1) % sections) for index in range(sections)]
    upper = [(index, (index + 1) % sections) for index in range(sections)]
    across = [(index, last - index) for index in range(sections)]
    upper_across = [(index, last - (index + 1) % sections) for index in range(sections)]

    h_first, h_later, h_up = local_call(
        normalize_body,
        [
            jax.ShapeDtypeStruct((2, shard_rows, features), jnp.bfloat16),
            jax.ShapeDtypeStruct((4, shard_rows, features), jnp.bfloat16),
            jax.ShapeDtypeStruct((TICKS, shard_rows, features), jnp.bfloat16),
        ],
        (x_down, x_up),
        flops=20 * x_up.size,
        moved=8 * x_up.size,
    )
    g_up = spread(flow_up)
    g_down = spread(flow_down)
    h0 = spread(h_first)
    later = lax.all_gather(h_later, "tp", axis=0, tiled=False)
    sent = lax.ppermute(jnp.concatenate([h_up, flow_up[None]], axis=0), "section", across)
    mirrored = lax.all_gather(sent, "tp", axis=0, tiled=False)

    saved_up = forward(h0, (1,), w_up)
    saved_down = forward(h0, (0,), w_down)
    flows, mirrored_flows, factors, mirrored_factors = [], [], [], []
    for tick in range(TICKS):
        if tick == 1:
            saved_up += forward(later, (2, 3), w_up)
            saved_down += forward(later, (0, 1), w_down)
        flows.append(g_down)
        final = tick + 1 == TICKS
        loss = min(tick, TICKS - 2)
        part_up, factor_up = backward(g_up, saved_up[tick], w_up, o_up)
        part_up = exchanged(part_up)
        mirrored_factors.append(lax.ppermute(factor_up, "section", across))
        part_down, factor_down = backward(g_down, saved_down[tick], w_down, o_down)
        part_down = exchanged(part_down)
        factors.append(factor_down)
        y_up = layer_back(
            part_up, x_up[tick], flow_up, ascending_loss_gradient[loss], None if final else last
        )
        y_down = layer_back(
            part_down, x_down[tick], flow_down, descending_loss_gradient[loss], None if final else 0
        )
        if not final:
            flow_up = lax.ppermute(y_up, "section", upper)
            flow_down = lax.ppermute(y_down, "section", lower)
            g_up = spread(flow_up)
            g_down = spread(flow_down)
            mirrored_flows.append(spread(lax.ppermute(y_up, "section", upper_across)))
    grad_qkv, grad_out = gradients(
        h0[:, :1], later, mirrored, flows, mirrored_flows, factors, mirrored_factors
    )
    return (
        jnp.transpose(grad_qkv, (1, 0, 2))[None],
        grad_out[None],
        y_down[None],
        y_up[None],
    )


def solution(mesh):
    in_specs = (
        P("section", None, None, "tp"),
        P("section", "tp", None),
        P("section", None, None, "tp"),
        P("section", "tp", None),
        P("section", None, "tp", None),
        P("section", None, "tp", None),
        P("section", "tp", None),
        P("section", "tp", None),
        P(None, "tp", None),
        P(None, "tp", None),
    )
    out_specs = (
        P("section", None, None, "tp"),
        P("section", "tp", None),
        P("section", "tp", None),
        P("section", "tp", None),
    )
    return jax.shard_map(
        per_device, mesh=mesh, in_specs=in_specs, out_specs=out_specs, check_vma=False
    )
```

```python
import functools

import jax
import jax.numpy as jnp
from jax import lax
from jax.experimental import pallas as pl
from jax.experimental.pallas import tpu as pltpu
from jax.sharding import PartitionSpec as P

HEAD = 128
TICKS = 3
EPSILON = 1e-05
MIB = 1 << 20
VMEM = pl.BlockSpec(memory_space=pltpu.VMEM)
ANY = pl.BlockSpec(memory_space=pl.ANY)
ROOM = 56 * MIB
CHUNK = 256


def dot_nn(left, right):
    return jnp.dot(left, right, preferred_element_type=jnp.float32)


def dot_nt(left, right):
    return lax.dot_general(left, right, (((1,), (1,)), ((), ())), preferred_element_type=jnp.float32)


def dot_tn(left, right):
    return lax.dot_general(left, right, (((0,), (0,)), ((), ())), preferred_element_type=jnp.float32)


def normalized(raw):
    centre = raw - jnp.mean(raw, axis=-1, keepdims=True)
    inverse = lax.rsqrt(jnp.mean(centre * centre, axis=-1, keepdims=True) + EPSILON)
    return centre * inverse, inverse


def local_call(body, out_shape, operands, flops, moved, in_specs=None, out_specs=None, scratch=()):
    return pl.pallas_call(
        body,
        out_shape=out_shape,
        in_specs=in_specs or [VMEM] * len(operands),
        out_specs=out_specs or jax.tree.map(lambda _: VMEM, out_shape),
        scratch_shapes=list(scratch),
        compiler_params=pltpu.CompilerParams(vmem_limit_bytes=ROOM),
        cost_estimate=pl.CostEstimate(flops=flops // 1000, bytes_accessed=moved // 1000, transcendentals=0),
    )(*operands)


def prepare_body(down_ref, up_ref, g_down_ref, g_up_ref, start_ref, later_ref, across_ref, block, sem):
    down = normalized(down_ref[...].astype(jnp.float32))[0].astype(jnp.bfloat16)
    up = normalized(up_ref[...].astype(jnp.float32))[0].astype(jnp.bfloat16)
    block[0] = up[0]
    block[1] = g_up_ref[...]
    block[2] = down[0]
    block[3] = g_down_ref[...]
    copies = [
        pltpu.make_async_copy(block, start_ref.at[shard], sem.at[shard])
        for shard in range(start_ref.shape[0])
    ]
    for copy in copies:
        copy.start()
    later_ref[0] = down[1]
    later_ref[1] = down[2]
    later_ref[2] = up[1]
    later_ref[3] = up[2]
    for tick in range(TICKS):
        across_ref[tick] = up[tick]
    across_ref[TICKS] = g_up_ref[...]
    for copy in copies:
        copy.wait()


def prepare(x_down, x_up, flow_down, flow_up):
    shards = lax.axis_size("tp")
    four = (4,) + flow_up.shape
    return local_call(
        prepare_body,
        [
            jax.ShapeDtypeStruct((shards,) + four, jnp.bfloat16),
            jax.ShapeDtypeStruct(four, jnp.bfloat16),
            jax.ShapeDtypeStruct(four, jnp.bfloat16),
        ],
        (x_down, x_up, flow_down, flow_up),
        flops=40 * x_up.size,
        moved=10 * x_up.size,
        out_specs=[ANY, VMEM, VMEM],
        scratch=[pltpu.VMEM(four, jnp.bfloat16), pltpu.SemaphoreType.DMA((shards,))],
    )


def repeat_body(*refs):
    sources, out_ref, sem = refs[:-2], refs[-2], refs[-1]
    copies = []
    for index, source in enumerate(sources):
        for shard in range(out_ref.shape[0]):
            copies.append(
                pltpu.make_async_copy(source, out_ref.at[shard, index], sem.at[index, shard])
            )
    for copy in copies:
        copy.start()
    for copy in copies:
        copy.wait()


def repeat(*rows):
    shards = lax.axis_size("tp")
    count = len(rows)
    return local_call(
        repeat_body,
        jax.ShapeDtypeStruct((shards, count) + rows[0].shape, jnp.bfloat16),
        rows,
        flops=rows[0].size,
        moved=16 * shards * rows[0].size,
        out_specs=ANY,
        scratch=[pltpu.SemaphoreType.DMA((count, shards))],
    )


def forward_body(picks, h_hbm, *refs):
    count = len(picks[0])
    weights, outs, (h_all, w_all, sem) = refs[:2], refs[2:-3], refs[-3:]
    features, local = w_all.shape[2:]
    rows = h_all.shape[2] * h_all.shape[3]
    h_copies = [
        [
            pltpu.make_async_copy(h_hbm.at[:, pick], h_all.at[pipe, index], sem.at[pipe, index])
            for index, pick in enumerate(picks[pipe])
        ]
        for pipe in range(2)
    ]
    w_copies = [
        [
            pltpu.make_async_copy(weights[pipe].at[part], w_all.at[pipe, part], sem.at[pipe, count + part])
            for part in range(3)
        ]
        for pipe in range(2)
    ]
    for pipe in range(2):
        for copy in h_copies[pipe] + w_copies[pipe]:
            copy.start()
    causal = lax.broadcasted_iota(jnp.int32, (rows, rows), 0) >= lax.broadcasted_iota(
        jnp.int32, (rows, rows), 1
    )
    for pipe in range(2):
        for copy in h_copies[pipe]:
            copy.wait()
        hidden = h_all[pipe].reshape(count * rows, features)
        projected = []
        for part in range(3):
            w_copies[pipe][part].wait()
            projected.append(dot_nn(hidden, w_all[pipe, part]).astype(jnp.bfloat16))
        queries, keys, values = projected
        for index in range(count):
            qkv_ref, soft_ref = outs[2 * index : 2 * index + 2]
            span = slice(index * rows, (index + 1) * rows)
            for part in range(3):
                qkv_ref[pipe, part] = projected[part][span]
            for head in range(local // HEAD):
                cols = slice(head * HEAD, (head + 1) * HEAD)
                scores = dot_nt(queries[span, cols], keys[span, cols]) * HEAD ** (-0.5)
                scores = jnp.where(causal, scores, -jnp.inf)
                powers = jnp.exp(scores - jnp.max(scores, axis=-1, keepdims=True))
                soft = powers / jnp.sum(powers, axis=-1, keepdims=True)
                soft_ref[pipe, head] = soft
                qkv_ref[pipe, 3, :, cols] = dot_nn(
                    soft.astype(jnp.bfloat16), values[span, cols]
                ).astype(jnp.bfloat16)


def forward(hidden, picks, w_up, w_down):
    shards, _, shard_rows, features = hidden.shape
    rows = shards * shard_rows
    local = w_up.shape[2]
    count = len(picks[0])
    outs = local_call(
        functools.partial(forward_body, picks),
        [
            jax.ShapeDtypeStruct((2, 4, rows, local), jnp.bfloat16),
            jax.ShapeDtypeStruct((2, local // HEAD, rows, rows), jnp.float32),
        ]
        * count,
        (hidden, w_up, w_down),
        flops=12 * count * rows * features * local,
        moved=8 * MIB,
        in_specs=[ANY] * 3,
        scratch=[
            pltpu.VMEM((2, count, shards, shard_rows, features), jnp.bfloat16),
            pltpu.VMEM((2, 3, features, local), jnp.bfloat16),
            pltpu.SemaphoreType.DMA((2, count + 3)),
        ],
    )
    return [outs[2 * index : 2 * index + 2] for index in range(count)]


def backward_body(picks, extra, g_hbm, qkv_hbm, soft_hbm, w_up, w_down, o_up, o_down, *rest):
    added, rest = rest[:extra], rest[extra:]
    part_hbm, factor_up, factor_down = rest[:3]
    g_all, qkv, soft_all, w_all, o_all, out, factor, sem, out_sem = rest[3:]
    shards, shard_rows, features = g_all.shape[1:]
    rows = shards * shard_rows
    local = o_all.shape[1]
    tile = 512
    copy = pltpu.make_async_copy
    first, second = [], []
    for pipe in range(2):
        first.append(
            [
                copy(g_hbm.at[:, picks[pipe]], g_all.at[pipe], sem.at[pipe, 0]),
                copy((o_up, o_down)[pipe], o_all.at[pipe], sem.at[pipe, 1]),
                copy(qkv_hbm.at[pipe], qkv.at[pipe], sem.at[pipe, 2]),
                copy(soft_hbm.at[pipe], soft_all.at[pipe], sem.at[pipe, 3]),
            ]
        )
        second.append([copy((w_up, w_down)[pipe], w_all.at[pipe], sem.at[pipe, 4])])
    for group in first + second:
        for one in group:
            one.start()
    pieces = []
    sent = [
        copy(row, part_hbm.at[shard, 2], out_sem.at[0, 1 + features // tile + shard])
        for row in added
        for shard in range(shards)
    ]
    for one in sent:
        one.start()
    for pipe in range(2):
        for one in first[pipe]:
            one.wait()
        upstream = g_all[pipe].reshape(rows, features)
        d_attended = dot_nt(upstream, o_all[pipe]).astype(jnp.bfloat16)
        d_queries, d_keys, d_values = [], [], []
        for head in range(local // HEAD):
            cols = slice(head * HEAD, (head + 1) * HEAD)
            queries, keys, values, attended = [qkv[pipe, part, :, cols] for part in range(4)]
            soft = soft_all[pipe, head]
            d_here = d_attended[:, cols]
            d_values.append(dot_tn(soft.astype(jnp.bfloat16), d_here).astype(jnp.bfloat16))
            d_probs = dot_nt(d_here, values)
            offset = jnp.sum(
                d_here.astype(jnp.float32) * attended.astype(jnp.float32), axis=-1, keepdims=True
            )
            d_scores = (soft * (d_probs - offset) * HEAD ** (-0.5)).astype(jnp.bfloat16)
            d_queries.append(dot_nn(d_scores, keys).astype(jnp.bfloat16))
            d_keys.append(dot_tn(d_scores, queries).astype(jnp.bfloat16))
        pieces.append([jnp.concatenate(parts, axis=1) for parts in (d_queries, d_keys, d_values)])
        for part in range(3):
            factor[pipe, part] = pieces[pipe][part]
        factor[pipe, 3] = qkv[pipe, 3]
        sent.append(copy(factor.at[pipe], (factor_up, factor_down)[pipe], out_sem.at[pipe, 0]))
        sent[-1].start()
    for pipe in range(2):
        for one in second[pipe]:
            one.wait()
        for index in range(features // tile):
            cols = slice(index * tile, (index + 1) * tile)
            total = dot_nt(pieces[pipe][0], w_all[pipe, 0, cols, :])
            total += dot_nt(pieces[pipe][1], w_all[pipe, 1, cols, :])
            total += dot_nt(pieces[pipe][2], w_all[pipe, 2, cols, :])
            out[pipe, :, :, cols] = total.astype(jnp.bfloat16).reshape(shards, shard_rows, tile)
            sent.append(
                copy(out.at[pipe, :, :, cols], part_hbm.at[:, pipe, :, cols], out_sem.at[pipe, 1 + index])
            )
            sent[-1].start()
    for one in sent:
        one.wait()


def backward(gathered, picks, saved, w_up, w_down, o_up, o_down, added):
    local, features = o_up.shape
    rows = saved[0].shape[2]
    shards = lax.axis_size("tp")
    wide = (shards, rows // shards, features)
    return local_call(
        functools.partial(backward_body, picks, len(added)),
        [
            jax.ShapeDtypeStruct((shards, 2 + len(added)) + wide[1:], jnp.bfloat16),
            jax.ShapeDtypeStruct((4, rows, local), jnp.bfloat16),
            jax.ShapeDtypeStruct((4, rows, local), jnp.bfloat16),
        ],
        (gathered, *saved, w_up, w_down, o_up, o_down, *added),
        flops=16 * rows * features * local,
        moved=12 * MIB,
        in_specs=[ANY] * 7 + [VMEM] * len(added),
        out_specs=[ANY] * 3,
        scratch=[
            pltpu.VMEM((2,) + wide, jnp.bfloat16),
            pltpu.VMEM((2, 4, rows, local), jnp.bfloat16),
            pltpu.VMEM((2, local // HEAD, rows, rows), jnp.float32),
            pltpu.VMEM((2, 3, features, local), jnp.bfloat16),
            pltpu.VMEM((2, local, features), jnp.bfloat16),
            pltpu.VMEM((2,) + wide, jnp.bfloat16),
            pltpu.VMEM((2, 4, rows, local), jnp.bfloat16),
            pltpu.SemaphoreType.DMA((2, 5)),
            pltpu.SemaphoreType.DMA((2, 1 + features // 512 + shards)),
        ],
    )


def layer_back_body(tick, ends, parts_ref, *refs):
    for pipe in range(2):
        x_ref, g_ref, loss_ref = refs[3 * pipe : 3 * pipe + 3]
        y_ref = refs[6 + pipe]
        summed = jnp.sum(parts_ref[:, pipe].astype(jnp.float32), axis=0)
        normed, inverse = normalized(x_ref[tick].astype(jnp.float32))
        backward = inverse * (
            summed
            - jnp.mean(summed, axis=-1, keepdims=True)
            - normed * jnp.mean(summed * normed, axis=-1, keepdims=True)
        )
        result = (g_ref[...].astype(jnp.float32) + backward).astype(jnp.bfloat16)
        if ends is not None:
            at_end = lax.axis_index("section") == ends[pipe]
            result = jnp.where(at_end, loss_ref[tick], result)
        y_ref[...] = result


def layer_back(parts, up, down, tick, ends):
    like = jax.ShapeDtypeStruct(up[1].shape, jnp.bfloat16)
    return local_call(
        functools.partial(layer_back_body, tick, ends),
        [like, like],
        (parts, *up, *down),
        flops=20 * parts.size,
        moved=3 * parts.size,
    )


def gradients_body(start, later, mirrored, g1, g2, moved, *rest):
    factors = rest[:6]
    w_ref, o_ref, d_all, a_all = rest[6:]
    rows = factors[0].shape[1]
    tile = start.shape[-1]

    @pl.when(pl.program_id(0) == 0)
    def _():
        for index, factor in enumerate(factors):
            for part in range(3):
                d_all[part, index * rows : (index + 1) * rows, :] = factor[part]
            a_all[:, index * rows : (index + 1) * rows] = factor[3].T

    def flat(block):
        return block.reshape(rows, tile)

    hidden = jnp.concatenate(
        [flat(start[:, 0]), flat(later[:, 0]), flat(later[:, 1])]
        + [flat(mirrored[:, index]) for index in range(TICKS)],
        axis=0,
    )
    upstream = jnp.concatenate(
        [flat(start[:, 1]), flat(g1[:, 0]), flat(g2[:, 0])]
        + [flat(mirrored[:, TICKS]), flat(mirrored[:, TICKS + 1]), flat(moved[:, 0])],
        axis=0,
    )
    turned = hidden.T
    for part in range(3):
        w_ref[part] = dot_nn(turned, d_all[part]).astype(jnp.bfloat16)
    o_ref[...] = dot_nn(a_all[...], upstream).astype(jnp.bfloat16)


def gradients(start, later, mirrored, gathered, moved, factors):
    features = start.shape[-1]
    rows, local = factors[0].shape[1:]
    tile = 256
    shards = start.shape[0]
    shard_rows = start.shape[2]

    def columns(count, at=0):
        return pl.BlockSpec((shards, count, shard_rows, tile), lambda i: (0, at, 0, i))

    whole = pl.BlockSpec((4, rows, local), lambda i: (0, 0, 0))
    depth = 2 * TICKS * rows
    return pl.pallas_call(
        gradients_body,
        grid=(features // tile,),
        out_shape=[
            jax.ShapeDtypeStruct((3, features, local), jnp.bfloat16),
            jax.ShapeDtypeStruct((local, features), jnp.bfloat16),
        ],
        in_specs=[columns(2, 1), columns(2), columns(TICKS + 2), columns(1, 1), columns(1, 1), columns(1, 2)] + [whole] * 6,
        out_specs=[
            pl.BlockSpec((3, tile, local), lambda i: (0, i, 0)),
            pl.BlockSpec((local, tile), lambda i: (0, i)),
        ],
        scratch_shapes=[
            pltpu.VMEM((3, depth, local), jnp.bfloat16),
            pltpu.VMEM((local, depth), jnp.bfloat16),
        ],
        compiler_params=pltpu.CompilerParams(vmem_limit_bytes=ROOM),
        cost_estimate=pl.CostEstimate(
            flops=2 * depth * features * 4 * local, bytes_accessed=12 * MIB, transcendentals=0
        ),
    )(start, later, mirrored, *gathered, moved, *factors)


def after(value, *others):
    return lax.optimization_barrier((value,) + others)[0]


def exchanged(parts):
    return lax.all_to_all(parts, "tp", split_axis=0, concat_axis=0, tiled=True)


def gathered_rows(rows):
    return lax.all_gather(rows, "tp", axis=0, tiled=False)


def per_device(
    query_key_value_weight,
    output_weight,
    ascending_query_key_value_weight,
    ascending_output_weight,
    descending_saved_input,
    ascending_saved_input,
    descending_transit_gradient,
    ascending_transit_gradient,
    descending_loss_gradient,
    ascending_loss_gradient,
):
    sections = lax.axis_size("section")
    last = sections - 1
    w_down = jnp.transpose(query_key_value_weight[0], (1, 0, 2))
    w_up = jnp.transpose(ascending_query_key_value_weight[0], (1, 0, 2))
    o_down = output_weight[0]
    o_up = ascending_output_weight[0]
    x_down = descending_saved_input[0]
    x_up = ascending_saved_input[0]
    flow_down = descending_transit_gradient[0]
    flow_up = ascending_transit_gradient[0]

    lower = [(index, (index - 1) % sections) for index in range(sections)]
    upper = [(index, (index + 1) % sections) for index in range(sections)]
    across = [(index, last - index) for index in range(sections)]

    start, h_later, sent = prepare(x_down, x_up, flow_down, flow_up)
    start = exchanged(start)
    start, h_later, sent = lax.optimization_barrier((start, h_later, sent))
    later = gathered_rows(h_later)
    sent = lax.ppermute(sent, "section", across)

    saved = forward(start, ((0,), (2,)), w_up, w_down)
    gathered, picks = start, (1, 3)
    flows, added, factors, mirrored_factors = [], [], [], []
    for tick in range(TICKS):
        final = tick + 1 == TICKS
        parts, factor_up, factor_down = backward(
            gathered, picks, saved[tick], w_up, w_down, o_up, o_down, added
        )
        factors.append(factor_down)
        if tick == 0:
            parts, sent = lax.optimization_barrier((parts, sent))
        else:
            parts, mirrored_factors[-1] = lax.optimization_barrier((parts, mirrored_factors[-1]))
        if tick == 1:
            parts, row_up = lax.optimization_barrier((parts, row_up))
            mirrored = gathered_rows(jnp.concatenate([sent, row_up[None]], axis=0))
        parts = exchanged(parts)
        y_up, y_down = layer_back(
            parts,
            (x_up, flow_up, ascending_loss_gradient),
            (x_down, flow_down, descending_loss_gradient),
            tick,
            None if final else (last, 0),
        )
        if not final:
            flow_up = lax.ppermute(y_up, "section", upper)
            flow_down = lax.ppermute(y_down, "section", lower)
            gathered = repeat(flow_up, flow_down)
            gathered, row_up = lax.optimization_barrier((gathered, flow_up))
            gathered = exchanged(gathered)
            picks = (0, 1)
            flows.append(gathered)
            if tick == 0:
                saved += forward(later, ((2, 3), (0, 1)), w_up, w_down)
                gathered, row_up, factor_up, saved[1:] = lax.optimization_barrier(
                    (gathered, row_up, factor_up, saved[1:])
                )
                row_up = lax.ppermute(row_up, "section", across)
            else:
                row_up = lax.ppermute(row_up, "section", across)
                gathered, factor_up, row_up = lax.optimization_barrier((gathered, factor_up, row_up))
                added = [row_up]
        mirrored_factors.append(lax.ppermute(factor_up, "section", across))
    factors += mirrored_factors
    grad_qkv, grad_out = gradients(start, later, mirrored, flows, parts, factors)
    return (
        jnp.transpose(grad_qkv, (1, 0, 2))[None],
        grad_out[None],
        y_down[None],
        y_up[None],
    )


def solution(mesh):
    in_specs = (
        P("section", None, None, "tp"),
        P("section", "tp", None),
        P("section", None, None, "tp"),
        P("section", "tp", None),
        P("section", None, "tp", None),
        P("section", None, "tp", None),
        P("section", "tp", None),
        P("section", "tp", None),
        P(None, "tp", None),
        P(None, "tp", None),
    )
    out_specs = (
        P("section", None, None, "tp"),
        P("section", "tp", None),
        P("section", "tp", None),
        P("section", "tp", None),
    )
    return jax.shard_map(
        per_device, mesh=mesh, in_specs=in_specs, out_specs=out_specs, check_vma=False
    )
```

```python
import functools

import jax
import jax.numpy as jnp
from jax import lax
from jax.experimental import pallas as pl
from jax.experimental.pallas import tpu as pltpu
from jax.sharding import PartitionSpec as P

HEAD = 128
TICKS = 3
EPSILON = 1e-05
MIB = 1 << 20
VMEM = pl.BlockSpec(memory_space=pltpu.VMEM)
ANY = pl.BlockSpec(memory_space=pl.ANY)
ROOM = 56 * MIB
CHUNK = 256


def dot_nn(left, right):
    return jnp.dot(left, right, preferred_element_type=jnp.float32)


def dot_nt(left, right):
    return lax.dot_general(left, right, (((1,), (1,)), ((), ())), preferred_element_type=jnp.float32)


def dot_tn(left, right):
    return lax.dot_general(left, right, (((0,), (0,)), ((), ())), preferred_element_type=jnp.float32)


def normalized(raw):
    centre = raw - jnp.mean(raw, axis=-1, keepdims=True)
    inverse = lax.rsqrt(jnp.mean(centre * centre, axis=-1, keepdims=True) + EPSILON)
    return centre * inverse, inverse


def local_call(body, out_shape, operands, flops, moved, in_specs=None, out_specs=None, scratch=()):
    return pl.pallas_call(
        body,
        out_shape=out_shape,
        in_specs=in_specs or [VMEM] * len(operands),
        out_specs=out_specs or jax.tree.map(lambda _: VMEM, out_shape),
        scratch_shapes=list(scratch),
        compiler_params=pltpu.CompilerParams(vmem_limit_bytes=ROOM),
        cost_estimate=pl.CostEstimate(flops=flops // 1000, bytes_accessed=moved // 1000, transcendentals=0),
    )(*operands)


def prepare_body(down_ref, up_ref, g_down_ref, g_up_ref, start_ref, later_ref, across_ref, block, sem):
    down = normalized(down_ref[...].astype(jnp.float32))[0].astype(jnp.bfloat16)
    up = normalized(up_ref[...].astype(jnp.float32))[0].astype(jnp.bfloat16)
    block[0] = up[0]
    block[1] = g_up_ref[...]
    block[2] = down[0]
    block[3] = g_down_ref[...]
    copies = [
        pltpu.make_async_copy(block, start_ref.at[shard], sem.at[shard])
        for shard in range(start_ref.shape[0])
    ]
    for copy in copies:
        copy.start()
    later_ref[0] = down[1]
    later_ref[1] = down[2]
    later_ref[2] = up[1]
    later_ref[3] = up[2]
    for tick in range(TICKS):
        across_ref[tick] = up[tick]
    across_ref[TICKS] = g_up_ref[...]
    for copy in copies:
        copy.wait()


def prepare(x_down, x_up, flow_down, flow_up):
    shards = lax.axis_size("tp")
    four = (4,) + flow_up.shape
    return local_call(
        prepare_body,
        [
            jax.ShapeDtypeStruct((shards,) + four, jnp.bfloat16),
            jax.ShapeDtypeStruct(four, jnp.bfloat16),
            jax.ShapeDtypeStruct(four, jnp.bfloat16),
        ],
        (x_down, x_up, flow_down, flow_up),
        flops=40 * x_up.size,
        moved=10 * x_up.size,
        out_specs=[ANY, VMEM, VMEM],
        scratch=[pltpu.VMEM(four, jnp.bfloat16), pltpu.SemaphoreType.DMA((shards,))],
    )


def repeat_body(*refs):
    sources, out_ref, sem = refs[:-2], refs[-2], refs[-1]
    copies = []
    for index, source in enumerate(sources):
        for shard in range(out_ref.shape[0]):
            copies.append(
                pltpu.make_async_copy(source, out_ref.at[shard, index], sem.at[index, shard])
            )
    for copy in copies:
        copy.start()
    for copy in copies:
        copy.wait()


def repeat(*rows):
    shards = lax.axis_size("tp")
    count = len(rows)
    return local_call(
        repeat_body,
        jax.ShapeDtypeStruct((shards, count) + rows[0].shape, jnp.bfloat16),
        rows,
        flops=rows[0].size,
        moved=16 * shards * rows[0].size,
        out_specs=ANY,
        scratch=[pltpu.SemaphoreType.DMA((count, shards))],
    )


def forward_body(picks, h_hbm, *refs):
    count = len(picks[0])
    weights, outs, (h_all, w_all, sem) = refs[:2], refs[2:-3], refs[-3:]
    features, local = w_all.shape[2:]
    rows = h_all.shape[2] * h_all.shape[3]
    h_copies = [
        [
            pltpu.make_async_copy(h_hbm.at[:, pick], h_all.at[pipe, index], sem.at[pipe, index])
            for index, pick in enumerate(picks[pipe])
        ]
        for pipe in range(2)
    ]
    w_copies = [
        [
            pltpu.make_async_copy(weights[pipe].at[part], w_all.at[pipe, part], sem.at[pipe, count + part])
            for part in range(3)
        ]
        for pipe in range(2)
    ]
    for pipe in range(2):
        for copy in h_copies[pipe] + w_copies[pipe]:
            copy.start()
    causal = lax.broadcasted_iota(jnp.int32, (rows, rows), 0) >= lax.broadcasted_iota(
        jnp.int32, (rows, rows), 1
    )
    projected = []
    for pipe in range(2):
        for copy in h_copies[pipe]:
            copy.wait()
        hidden = h_all[pipe].reshape(count * rows, features)
        for part in range(3):
            w_copies[pipe][part].wait()
            projected.append(dot_nn(hidden, w_all[pipe, part]).astype(jnp.bfloat16))
    places = [
        (pipe, index, head, slice(index * rows, (index + 1) * rows), slice(head * HEAD, (head + 1) * HEAD))
        for pipe in range(2)
        for index in range(count)
        for head in range(local // HEAD)
    ]
    scores = [
        dot_nt(projected[3 * pipe][span, cols], projected[3 * pipe + 1][span, cols])
        for pipe, _, _, span, cols in places
    ]
    scores = [jnp.where(causal, score * HEAD ** (-0.5), -jnp.inf) for score in scores]
    powers = [jnp.exp(score - jnp.max(score, axis=-1, keepdims=True)) for score in scores]
    softs = [power / jnp.sum(power, axis=-1, keepdims=True) for power in powers]
    mixed = [
        dot_nn(soft.astype(jnp.bfloat16), projected[3 * pipe + 2][span, cols]).astype(jnp.bfloat16)
        for soft, (pipe, _, _, span, cols) in zip(softs, places)
    ]
    for pipe in range(2):
        for index in range(count):
            span = slice(index * rows, (index + 1) * rows)
            for part in range(3):
                outs[2 * index][pipe, part] = projected[3 * pipe + part][span]
    for soft, mix, (pipe, index, head, _, cols) in zip(softs, mixed, places):
        outs[2 * index + 1][pipe, head] = soft
        outs[2 * index][pipe, 3, :, cols] = mix


def forward(hidden, picks, w_up, w_down):
    shards, _, shard_rows, features = hidden.shape
    rows = shards * shard_rows
    local = w_up.shape[2]
    count = len(picks[0])
    outs = local_call(
        functools.partial(forward_body, picks),
        [
            jax.ShapeDtypeStruct((2, 4, rows, local), jnp.bfloat16),
            jax.ShapeDtypeStruct((2, local // HEAD, rows, rows), jnp.float32),
        ]
        * count,
        (hidden, w_up, w_down),
        flops=12 * count * rows * features * local,
        moved=8 * MIB,
        in_specs=[ANY] * 3,
        scratch=[
            pltpu.VMEM((2, count, shards, shard_rows, features), jnp.bfloat16),
            pltpu.VMEM((2, 3, features, local), jnp.bfloat16),
            pltpu.SemaphoreType.DMA((2, count + 3)),
        ],
    )
    return [outs[2 * index : 2 * index + 2] for index in range(count)]


def backward_body(picks, extra, g_hbm, qkv_hbm, soft_hbm, w_up, w_down, o_up, o_down, *rest):
    added, rest = rest[:extra], rest[extra:]
    part_hbm, factor_up, factor_down = rest[:3]
    g_all, qkv, soft_all, w_all, o_all, out, factor, sem, out_sem = rest[3:]
    shards, shard_rows, features = g_all.shape[1:]
    rows = shards * shard_rows
    local = o_all.shape[1]
    tile = 1024
    copy = pltpu.make_async_copy
    first, second = [], []
    for pipe in range(2):
        first.append(
            [
                copy(g_hbm.at[:, picks[pipe]], g_all.at[pipe], sem.at[pipe, 0]),
                copy((o_up, o_down)[pipe], o_all.at[pipe], sem.at[pipe, 1]),
                copy(qkv_hbm.at[pipe], qkv.at[pipe], sem.at[pipe, 2]),
                copy(soft_hbm.at[pipe], soft_all.at[pipe], sem.at[pipe, 3]),
            ]
        )
        second.append([copy((w_up, w_down)[pipe].at[part, pl.ds(half * 1024, 1024)], w_all.at[pipe, part, pl.ds(half * 1024, 1024)], sem.at[pipe, 4 + 2 * part + half]) for part in range(3) for half in range(2)])
    for group in first + second:
        for one in group:
            one.start()
    pieces = []
    sent = [
        copy(row, part_hbm.at[shard, 2], out_sem.at[0, 1 + features // tile + shard])
        for row in added
        for shard in range(shards)
    ]
    for one in sent:
        one.start()
    arrived = []
    for pipe in range(2):
        for one in first[pipe]:
            one.wait()
        upstream = g_all[pipe].reshape(rows, features)
        arrived.append(dot_nt(upstream, o_all[pipe]).astype(jnp.bfloat16))
    heads = [(pipe, head, slice(head * HEAD, (head + 1) * HEAD)) for pipe in range(2) for head in range(local // HEAD)]
    here = [arrived[pipe][:, cols] for pipe, _, cols in heads]
    d_probs = [dot_nt(d_here, qkv[pipe, 2, :, cols]) for d_here, (pipe, _, cols) in zip(here, heads)]
    offsets = [
        jnp.sum(d_here.astype(jnp.float32) * qkv[pipe, 3, :, cols].astype(jnp.float32), axis=-1, keepdims=True)
        for d_here, (pipe, _, cols) in zip(here, heads)
    ]
    softs = [soft_all[pipe, head] for pipe, head, _ in heads]
    d_scores = [
        (soft * (d_prob - offset) * HEAD ** (-0.5)).astype(jnp.bfloat16)
        for soft, d_prob, offset in zip(softs, d_probs, offsets)
    ]
    for soft, d_here, d_score, (pipe, _, cols) in zip(softs, here, d_scores, heads):
        factor[pipe, 0, :, cols] = dot_nn(d_score, qkv[pipe, 1, :, cols]).astype(jnp.bfloat16)
        factor[pipe, 1, :, cols] = dot_tn(d_score, qkv[pipe, 0, :, cols]).astype(jnp.bfloat16)
        factor[pipe, 2, :, cols] = dot_tn(soft.astype(jnp.bfloat16), d_here).astype(jnp.bfloat16)
    for pipe in range(2):
        factor[pipe, 3] = qkv[pipe, 3]
        sent.append(copy(factor.at[pipe], (factor_up, factor_down)[pipe], out_sem.at[pipe, 0]))
        sent[-1].start()
    pieces = [[factor[pipe, part] for part in range(3)] for pipe in range(2)]
    for pipe in range(2):
        for one in second[pipe]:
            one.wait()
        for index in range(features // tile):
            cols = slice(index * tile, (index + 1) * tile)
            total = dot_nt(pieces[pipe][0], w_all[pipe, 0, cols, :])
            total += dot_nt(pieces[pipe][1], w_all[pipe, 1, cols, :])
            total += dot_nt(pieces[pipe][2], w_all[pipe, 2, cols, :])
            out[pipe, :, :, cols] = total.astype(jnp.bfloat16).reshape(shards, shard_rows, tile)
            sent.append(
                copy(out.at[pipe, :, :, cols], part_hbm.at[:, pipe, :, cols], out_sem.at[pipe, 1 + index])
            )
            sent[-1].start()
    for one in sent:
        one.wait()


def backward(gathered, picks, saved, w_up, w_down, o_up, o_down, added):
    local, features = o_up.shape
    rows = saved[0].shape[2]
    shards = lax.axis_size("tp")
    wide = (shards, rows // shards, features)
    return local_call(
        functools.partial(backward_body, picks, len(added)),
        [
            jax.ShapeDtypeStruct((shards, 2 + len(added)) + wide[1:], jnp.bfloat16),
            jax.ShapeDtypeStruct((4, rows, local), jnp.bfloat16),
            jax.ShapeDtypeStruct((4, rows, local), jnp.bfloat16),
        ],
        (gathered, *saved, w_up, w_down, o_up, o_down, *added),
        flops=16 * rows * features * local,
        moved=12 * MIB,
        in_specs=[ANY] * 7 + [VMEM] * len(added),
        out_specs=[ANY] * 3,
        scratch=[
            pltpu.VMEM((2,) + wide, jnp.bfloat16),
            pltpu.VMEM((2, 4, rows, local), jnp.bfloat16),
            pltpu.VMEM((2, local // HEAD, rows, rows), jnp.float32),
            pltpu.VMEM((2, 3, features, local), jnp.bfloat16),
            pltpu.VMEM((2, local, features), jnp.bfloat16),
            pltpu.VMEM((2,) + wide, jnp.bfloat16),
            pltpu.VMEM((2, 4, rows, local), jnp.bfloat16),
            pltpu.SemaphoreType.DMA((2, 10)),
            pltpu.SemaphoreType.DMA((2, 1 + features // 1024 + shards)),
        ],
    )


def layer_back_body(tick, ends, parts_ref, *refs):
    for pipe in range(2):
        x_ref, g_ref, loss_ref = refs[3 * pipe : 3 * pipe + 3]
        y_ref = refs[6 + pipe]
        summed = jnp.sum(parts_ref[:, pipe].astype(jnp.float32), axis=0)
        normed, inverse = normalized(x_ref[tick].astype(jnp.float32))
        backward = inverse * (
            summed
            - jnp.mean(summed, axis=-1, keepdims=True)
            - normed * jnp.mean(summed * normed, axis=-1, keepdims=True)
        )
        result = (g_ref[...].astype(jnp.float32) + backward).astype(jnp.bfloat16)
        if ends is not None:
            at_end = lax.axis_index("section") == ends[pipe]
            result = jnp.where(at_end, loss_ref[tick], result)
        y_ref[...] = result


def layer_back(parts, up, down, tick, ends):
    like = jax.ShapeDtypeStruct(up[1].shape, jnp.bfloat16)
    return local_call(
        functools.partial(layer_back_body, tick, ends),
        [like, like],
        (parts, *up, *down),
        flops=20 * parts.size,
        moved=3 * parts.size,
    )


def qkv_gradient_body(start, later, mirrored, *rest):
    factors, (w_ref, d_all) = rest[:6], rest[6:]
    rows = factors[0].shape[1]
    tile = start.shape[-1]

    @pl.when(pl.program_id(0) == 0)
    def _():
        for index, factor in enumerate(factors):
            for part in range(3):
                d_all[part, index * rows : (index + 1) * rows, :] = factor[part]

    def flat(block):
        return block.reshape(rows, tile)

    hidden = jnp.concatenate(
        [flat(start[:, 0]), flat(later[:, 0]), flat(later[:, 1])]
        + [flat(mirrored[:, index]) for index in range(TICKS)],
        axis=0,
    )
    turned = hidden.T
    for part in range(3):
        w_ref[part] = dot_nn(turned, d_all[part]).astype(jnp.bfloat16)


def qkv_gradient(start, later, mirrored, factors):
    shards, _, shard_rows, features = start.shape
    rows, local = factors[0].shape[1:]
    tile = 256

    def columns(count, at=0):
        return pl.BlockSpec((shards, count, shard_rows, tile), lambda i: (0, at, 0, i))

    whole = pl.BlockSpec((3, rows, local), lambda i: (0, 0, 0))
    depth = 2 * TICKS * rows
    return pl.pallas_call(
        qkv_gradient_body,
        grid=(features // tile,),
        out_shape=jax.ShapeDtypeStruct((3, features, local), jnp.bfloat16),
        in_specs=[columns(1, 2), columns(2), columns(TICKS)] + [whole] * 6,
        out_specs=pl.BlockSpec((3, tile, local), lambda i: (0, i, 0)),
        scratch_shapes=[pltpu.VMEM((3, depth, local), jnp.bfloat16)],
        compiler_params=pltpu.CompilerParams(vmem_limit_bytes=ROOM),
        cost_estimate=pl.CostEstimate(
            flops=600 * depth * features * local, bytes_accessed=800 * MIB, transcendentals=0
        ),
    )(start, later, mirrored, *factors)


def out_gradient_body(picks, *refs):
    flows, factors = refs[: len(picks)], refs[len(picks) : 2 * len(picks)]
    out_hbm, g_all, a_all, result, sem, out_sem = refs[2 * len(picks) :]
    copy = pltpu.make_async_copy
    copies = []
    for index, pick in enumerate(picks):
        copies.append(copy(factors[index].at[3], a_all.at[index], sem.at[0, index]))
        copies.append(copy(flows[index].at[:, pick], g_all.at[index], sem.at[1, index]))
    for one in copies:
        one.start()
    for one in copies:
        one.wait()
    rows, local = a_all.shape[1:]
    features = g_all.shape[-1]
    turned = a_all[...].reshape(len(picks) * rows, local).T
    tile = features // 2
    sent = []
    for index in range(2):
        cols = slice(index * tile, (index + 1) * tile)
        upstream = g_all[:, :, :, cols].reshape(len(picks) * rows, tile)
        result[:, cols] = dot_nn(turned, upstream).astype(jnp.bfloat16)
        sent.append(copy(result.at[:, cols], out_hbm.at[:, cols], out_sem.at[index]))
        sent[-1].start()
    for one in sent:
        one.wait()


def out_gradient(flows, picks, factors):
    shards, _, shard_rows, features = flows[0].shape
    rows, local = factors[0].shape[1:]
    count = len(picks)
    return local_call(
        functools.partial(out_gradient_body, picks),
        jax.ShapeDtypeStruct((local, features), jnp.bfloat16),
        (*flows, *factors),
        flops=2 * count * rows * features * local,
        moved=5 * MIB,
        in_specs=[ANY] * (2 * count),
        out_specs=ANY,
        scratch=[
            pltpu.VMEM((count, shards, shard_rows, features), jnp.bfloat16),
            pltpu.VMEM((count, rows, local), jnp.bfloat16),
            pltpu.VMEM((local, features), jnp.bfloat16),
            pltpu.SemaphoreType.DMA((2, count)),
            pltpu.SemaphoreType.DMA((2,)),
        ],
    )


def after(value, *others):
    return lax.optimization_barrier((value,) + others)[0]


def exchanged(parts):
    return lax.all_to_all(parts, "tp", split_axis=0, concat_axis=0, tiled=True)


def gathered_rows(rows):
    return lax.all_gather(rows, "tp", axis=0, tiled=False)


def per_device(
    query_key_value_weight,
    output_weight,
    ascending_query_key_value_weight,
    ascending_output_weight,
    descending_saved_input,
    ascending_saved_input,
    descending_transit_gradient,
    ascending_transit_gradient,
    descending_loss_gradient,
    ascending_loss_gradient,
):
    sections = lax.axis_size("section")
    last = sections - 1
    w_down = jnp.transpose(query_key_value_weight[0], (1, 0, 2))
    w_up = jnp.transpose(ascending_query_key_value_weight[0], (1, 0, 2))
    o_down = output_weight[0]
    o_up = ascending_output_weight[0]
    x_down = descending_saved_input[0]
    x_up = ascending_saved_input[0]
    flow_down = descending_transit_gradient[0]
    flow_up = ascending_transit_gradient[0]

    lower = [(index, (index - 1) % sections) for index in range(sections)]
    upper = [(index, (index + 1) % sections) for index in range(sections)]
    across = [(index, last - index) for index in range(sections)]

    start, h_later, sent = prepare(x_down, x_up, flow_down, flow_up)
    start = exchanged(start)
    start, h_later, sent = lax.optimization_barrier((start, h_later, sent))
    later = gathered_rows(h_later)
    sent = lax.ppermute(sent, "section", across)

    saved = forward(start, ((0,), (2,)), w_up, w_down)
    gathered, picks = start, (1, 3)
    flows, added, factors, mirrored_factors = [], [], [], []
    for tick in range(TICKS):
        final = tick + 1 == TICKS
        parts, factor_up, factor_down = backward(
            gathered, picks, saved[tick], w_up, w_down, o_up, o_down, added
        )
        factors.append(factor_down)
        if tick == 0:
            parts, sent = lax.optimization_barrier((parts, sent))
        else:
            parts, mirrored_factors[-1] = lax.optimization_barrier((parts, mirrored_factors[-1]))
        if tick == 1:
            parts, row_up = lax.optimization_barrier((parts, row_up))
            mirrored = gathered_rows(jnp.concatenate([sent, row_up[None]], axis=0))
        parts = exchanged(parts)
        if final:
            mirrored_factors.append(lax.ppermute(factor_up, "section", across))
            grad_qkv = qkv_gradient(start, later, mirrored, factors + mirrored_factors)
            parts, grad_qkv = lax.optimization_barrier((parts, grad_qkv))
        y_up, y_down = layer_back(
            parts,
            (x_up, flow_up, ascending_loss_gradient),
            (x_down, flow_down, descending_loss_gradient),
            tick,
            None if final else (last, 0),
        )
        if not final:
            flow_up = lax.ppermute(y_up, "section", upper)
            flow_down = lax.ppermute(y_down, "section", lower)
            gathered = repeat(flow_up, flow_down)
            gathered, row_up = lax.optimization_barrier((gathered, flow_up))
            gathered = exchanged(gathered)
            picks = (0, 1)
            flows.append(gathered)
            if tick == 0:
                saved += forward(later, ((2, 3), (0, 1)), w_up, w_down)
                gathered, row_up, factor_up, saved[1:] = lax.optimization_barrier(
                    (gathered, row_up, factor_up, saved[1:])
                )
                row_up = lax.ppermute(row_up, "section", across)
            else:
                row_up = lax.ppermute(row_up, "section", across)
                gathered, factor_up, row_up = lax.optimization_barrier((gathered, factor_up, row_up))
                added = [row_up]
            mirrored_factors.append(lax.ppermute(factor_up, "section", across))
    grad_out = out_gradient(
        (start, *flows, mirrored, mirrored, parts),
        (3, 1, 1, TICKS, TICKS + 1, 2),
        factors + mirrored_factors,
    )
    return (
        jnp.transpose(grad_qkv, (1, 0, 2))[None],
        grad_out[None],
        y_down[None],
        y_up[None],
    )


def solution(mesh):
    in_specs = (
        P("section", None, None, "tp"),
        P("section", "tp", None),
        P("section", None, None, "tp"),
        P("section", "tp", None),
        P("section", None, "tp", None),
        P("section", None, "tp", None),
        P("section", "tp", None),
        P("section", "tp", None),
        P(None, "tp", None),
        P(None, "tp", None),
    )
    out_specs = (
        P("section", None, None, "tp"),
        P("section", "tp", None),
        P("section", "tp", None),
        P("section", "tp", None),
    )
    return jax.shard_map(
        per_device, mesh=mesh, in_specs=in_specs, out_specs=out_specs, check_vma=False
    )
```

```python
import functools

import jax
import jax.numpy as jnp
from jax import lax
from jax.experimental import pallas as pl
from jax.experimental.pallas import tpu as pltpu
from jax.sharding import PartitionSpec as P

HEAD = 128
TICKS = 3
EPSILON = 1e-05
MIB = 1 << 20
VMEM = pl.BlockSpec(memory_space=pltpu.VMEM)
ANY = pl.BlockSpec(memory_space=pl.ANY)
ROOM = 56 * MIB
CHUNK = 256


def dot_nn(left, right):
    return jnp.dot(left, right, preferred_element_type=jnp.float32)


def dot_nt(left, right):
    return lax.dot_general(left, right, (((1,), (1,)), ((), ())), preferred_element_type=jnp.float32)


def dot_tn(left, right):
    return lax.dot_general(left, right, (((0,), (0,)), ((), ())), preferred_element_type=jnp.float32)


def normalized(raw):
    centre = raw - jnp.mean(raw, axis=-1, keepdims=True)
    inverse = lax.rsqrt(jnp.mean(centre * centre, axis=-1, keepdims=True) + EPSILON)
    return centre * inverse, inverse


def local_call(body, out_shape, operands, flops, moved, in_specs=None, out_specs=None, scratch=()):
    return pl.pallas_call(
        body,
        out_shape=out_shape,
        in_specs=in_specs or [VMEM] * len(operands),
        out_specs=out_specs or jax.tree.map(lambda _: VMEM, out_shape),
        scratch_shapes=list(scratch),
        compiler_params=pltpu.CompilerParams(vmem_limit_bytes=ROOM),
        cost_estimate=pl.CostEstimate(flops=flops // 1000, bytes_accessed=moved // 1000, transcendentals=0),
    )(*operands)


def prepare_body(down_ref, up_ref, g_down_ref, g_up_ref, start_ref, later_ref, across_ref, block, sem):
    down = normalized(down_ref[...].astype(jnp.float32))[0].astype(jnp.bfloat16)
    up = normalized(up_ref[...].astype(jnp.float32))[0].astype(jnp.bfloat16)
    block[0] = up[0]
    block[1] = g_up_ref[...]
    block[2] = down[0]
    block[3] = g_down_ref[...]
    copies = [
        pltpu.make_async_copy(block, start_ref.at[shard], sem.at[shard])
        for shard in range(start_ref.shape[0])
    ]
    for copy in copies:
        copy.start()
    later_ref[0] = down[1]
    later_ref[1] = down[2]
    later_ref[2] = up[1]
    later_ref[3] = up[2]
    for tick in range(TICKS):
        across_ref[tick] = up[tick]
    across_ref[TICKS] = g_up_ref[...]
    for copy in copies:
        copy.wait()


def prepare(x_down, x_up, flow_down, flow_up):
    shards = lax.axis_size("tp")
    four = (4,) + flow_up.shape
    return local_call(
        prepare_body,
        [
            jax.ShapeDtypeStruct((shards,) + four, jnp.bfloat16),
            jax.ShapeDtypeStruct(four, jnp.bfloat16),
            jax.ShapeDtypeStruct(four, jnp.bfloat16),
        ],
        (x_down, x_up, flow_down, flow_up),
        flops=40 * x_up.size,
        moved=10 * x_up.size,
        out_specs=[ANY, VMEM, VMEM],
        scratch=[pltpu.VMEM(four, jnp.bfloat16), pltpu.SemaphoreType.DMA((shards,))],
    )


def repeat_body(*refs):
    sources, out_ref, sem = refs[:-2], refs[-2], refs[-1]
    copies = []
    for index, source in enumerate(sources):
        for shard in range(out_ref.shape[0]):
            copies.append(
                pltpu.make_async_copy(source, out_ref.at[shard, index], sem.at[index, shard])
            )
    for copy in copies:
        copy.start()
    for copy in copies:
        copy.wait()


def repeat(*rows):
    shards = lax.axis_size("tp")
    count = len(rows)
    return local_call(
        repeat_body,
        jax.ShapeDtypeStruct((shards, count) + rows[0].shape, jnp.bfloat16),
        rows,
        flops=rows[0].size,
        moved=16 * shards * rows[0].size,
        out_specs=ANY,
        scratch=[pltpu.SemaphoreType.DMA((count, shards))],
    )


def forward_body(picks, h_hbm, *refs):
    count = len(picks[0])
    weights, outs, (h_all, w_all, sem) = refs[:2], refs[2:-3], refs[-3:]
    features, local = w_all.shape[2:]
    rows = h_all.shape[2] * h_all.shape[3]
    h_copies = [
        [
            pltpu.make_async_copy(h_hbm.at[:, pick], h_all.at[pipe, index], sem.at[pipe, index])
            for index, pick in enumerate(picks[pipe])
        ]
        for pipe in range(2)
    ]
    w_copies = [
        [
            pltpu.make_async_copy(weights[pipe].at[part], w_all.at[pipe, part], sem.at[pipe, count + part])
            for part in range(3)
        ]
        for pipe in range(2)
    ]
    for pipe in range(2):
        for copy in h_copies[pipe] + w_copies[pipe]:
            copy.start()
    causal = lax.broadcasted_iota(jnp.int32, (rows, rows), 0) >= lax.broadcasted_iota(
        jnp.int32, (rows, rows), 1
    )
    projected = []
    for pipe in range(2):
        for copy in h_copies[pipe]:
            copy.wait()
        hidden = h_all[pipe].reshape(count * rows, features)
        for part in range(3):
            w_copies[pipe][part].wait()
            projected.append(dot_nn(hidden, w_all[pipe, part]).astype(jnp.bfloat16))
    places = [
        (pipe, index, head, slice(index * rows, (index + 1) * rows), slice(head * HEAD, (head + 1) * HEAD))
        for pipe in range(2)
        for index in range(count)
        for head in range(local // HEAD)
    ]
    scores = [
        dot_nt(projected[3 * pipe][span, cols], projected[3 * pipe + 1][span, cols])
        for pipe, _, _, span, cols in places
    ]
    scores = [jnp.where(causal, score * HEAD ** (-0.5), -jnp.inf) for score in scores]
    powers = [jnp.exp(score - jnp.max(score, axis=-1, keepdims=True)) for score in scores]
    softs = [power / jnp.sum(power, axis=-1, keepdims=True) for power in powers]
    mixed = [
        dot_nn(soft.astype(jnp.bfloat16), projected[3 * pipe + 2][span, cols]).astype(jnp.bfloat16)
        for soft, (pipe, _, _, span, cols) in zip(softs, places)
    ]
    for pipe in range(2):
        for index in range(count):
            span = slice(index * rows, (index + 1) * rows)
            for part in range(3):
                outs[2 * index][pipe, part] = projected[3 * pipe + part][span]
    for soft, mix, (pipe, index, head, _, cols) in zip(softs, mixed, places):
        outs[2 * index + 1][pipe, head] = soft
        outs[2 * index][pipe, 3, :, cols] = mix


def forward(hidden, picks, w_up, w_down):
    shards, _, shard_rows, features = hidden.shape
    rows = shards * shard_rows
    local = w_up.shape[2]
    count = len(picks[0])
    outs = local_call(
        functools.partial(forward_body, picks),
        [
            jax.ShapeDtypeStruct((2, 4, rows, local), jnp.bfloat16),
            jax.ShapeDtypeStruct((2, local // HEAD, rows, rows), jnp.float32),
        ]
        * count,
        (hidden, w_up, w_down),
        flops=12 * count * rows * features * local,
        moved=8 * MIB,
        in_specs=[ANY] * 3,
        scratch=[
            pltpu.VMEM((2, count, shards, shard_rows, features), jnp.bfloat16),
            pltpu.VMEM((2, 3, features, local), jnp.bfloat16),
            pltpu.SemaphoreType.DMA((2, count + 3)),
        ],
    )
    return [outs[2 * index : 2 * index + 2] for index in range(count)]


def backward_body(picks, extra, g_hbm, qkv_hbm, soft_hbm, w_up, w_down, o_up, o_down, *rest):
    added, rest = rest[:extra], rest[extra:]
    part_hbm, factor_up, factor_down = rest[:3]
    g_all, qkv, soft_all, w_all, o_all, out, factor, sem, out_sem = rest[3:]
    shards, shard_rows, features = g_all.shape[1:]
    rows = shards * shard_rows
    local = o_all.shape[1]
    tile = 1024
    copy = pltpu.make_async_copy
    first, second = [], []
    for pipe in range(2):
        first.append(
            [
                copy(g_hbm.at[:, picks[pipe]], g_all.at[pipe], sem.at[pipe, 0]),
                copy((o_up, o_down)[pipe], o_all.at[pipe], sem.at[pipe, 1]),
                copy(qkv_hbm.at[pipe], qkv.at[pipe], sem.at[pipe, 2]),
                copy(soft_hbm.at[pipe], soft_all.at[pipe], sem.at[pipe, 3]),
            ]
        )
        second.append([copy((w_up, w_down)[pipe].at[part, pl.ds(half * 1024, 1024)], w_all.at[pipe, part, pl.ds(half * 1024, 1024)], sem.at[pipe, 4 + 2 * part + half]) for part in range(3) for half in range(2)])
    for group in first + second:
        for one in group:
            one.start()
    pieces = []
    sent = [
        copy(row, part_hbm.at[shard, 2], out_sem.at[0, 1 + features // tile + shard])
        for row in added
        for shard in range(shards)
    ]
    for one in sent:
        one.start()
    arrived = []
    for pipe in range(2):
        for one in first[pipe]:
            one.wait()
        upstream = g_all[pipe].reshape(rows, features)
        arrived.append(dot_nt(upstream, o_all[pipe]).astype(jnp.bfloat16))
    heads = [(pipe, head, slice(head * HEAD, (head + 1) * HEAD)) for pipe in range(2) for head in range(local // HEAD)]
    here = [arrived[pipe][:, cols] for pipe, _, cols in heads]
    d_probs = [dot_nt(d_here, qkv[pipe, 2, :, cols]) for d_here, (pipe, _, cols) in zip(here, heads)]
    offsets = [
        jnp.sum(d_here.astype(jnp.float32) * qkv[pipe, 3, :, cols].astype(jnp.float32), axis=-1, keepdims=True)
        for d_here, (pipe, _, cols) in zip(here, heads)
    ]
    softs = [soft_all[pipe, head] for pipe, head, _ in heads]
    d_scores = [
        (soft * (d_prob - offset) * HEAD ** (-0.5)).astype(jnp.bfloat16)
        for soft, d_prob, offset in zip(softs, d_probs, offsets)
    ]
    for soft, d_here, d_score, (pipe, _, cols) in zip(softs, here, d_scores, heads):
        factor[pipe, 0, :, cols] = dot_nn(d_score, qkv[pipe, 1, :, cols]).astype(jnp.bfloat16)
        factor[pipe, 1, :, cols] = dot_tn(d_score, qkv[pipe, 0, :, cols]).astype(jnp.bfloat16)
        factor[pipe, 2, :, cols] = dot_tn(soft.astype(jnp.bfloat16), d_here).astype(jnp.bfloat16)
    for pipe in range(2):
        factor[pipe, 3] = qkv[pipe, 3]
        sent.append(copy(factor.at[pipe], (factor_up, factor_down)[pipe], out_sem.at[pipe, 0]))
        sent[-1].start()
    pieces = [[factor[pipe, part] for part in range(3)] for pipe in range(2)]
    for pipe in range(2):
        for one in second[pipe]:
            one.wait()
        for index in range(features // tile):
            cols = slice(index * tile, (index + 1) * tile)
            total = dot_nt(pieces[pipe][0], w_all[pipe, 0, cols, :])
            total += dot_nt(pieces[pipe][1], w_all[pipe, 1, cols, :])
            total += dot_nt(pieces[pipe][2], w_all[pipe, 2, cols, :])
            out[pipe, :, :, cols] = total.astype(jnp.bfloat16).reshape(shards, shard_rows, tile)
            sent.append(
                copy(out.at[pipe, :, :, cols], part_hbm.at[:, pipe, :, cols], out_sem.at[pipe, 1 + index])
            )
            sent[-1].start()
    for one in sent:
        one.wait()


def backward(gathered, picks, saved, w_up, w_down, o_up, o_down, added):
    local, features = o_up.shape
    rows = saved[0].shape[2]
    shards = lax.axis_size("tp")
    wide = (shards, rows // shards, features)
    return local_call(
        functools.partial(backward_body, picks, len(added)),
        [
            jax.ShapeDtypeStruct((shards, 2 + len(added)) + wide[1:], jnp.bfloat16),
            jax.ShapeDtypeStruct((4, rows, local), jnp.bfloat16),
            jax.ShapeDtypeStruct((4, rows, local), jnp.bfloat16),
        ],
        (gathered, *saved, w_up, w_down, o_up, o_down, *added),
        flops=16 * rows * features * local,
        moved=12 * MIB,
        in_specs=[ANY] * 7 + [VMEM] * len(added),
        out_specs=[ANY] * 3,
        scratch=[
            pltpu.VMEM((2,) + wide, jnp.bfloat16),
            pltpu.VMEM((2, 4, rows, local), jnp.bfloat16),
            pltpu.VMEM((2, local // HEAD, rows, rows), jnp.float32),
            pltpu.VMEM((2, 3, features, local), jnp.bfloat16),
            pltpu.VMEM((2, local, features), jnp.bfloat16),
            pltpu.VMEM((2,) + wide, jnp.bfloat16),
            pltpu.VMEM((2, 4, rows, local), jnp.bfloat16),
            pltpu.SemaphoreType.DMA((2, 10)),
            pltpu.SemaphoreType.DMA((2, 1 + features // 1024 + shards)),
        ],
    )


def layer_back_body(tick, ends, parts_ref, *refs):
    for pipe in range(2):
        x_ref, g_ref, loss_ref = refs[3 * pipe : 3 * pipe + 3]
        y_ref = refs[6 + pipe]
        summed = jnp.sum(parts_ref[:, pipe].astype(jnp.float32), axis=0)
        normed, inverse = normalized(x_ref[tick].astype(jnp.float32))
        backward = inverse * (
            summed
            - jnp.mean(summed, axis=-1, keepdims=True)
            - normed * jnp.mean(summed * normed, axis=-1, keepdims=True)
        )
        result = (g_ref[...].astype(jnp.float32) + backward).astype(jnp.bfloat16)
        if ends is not None:
            at_end = lax.axis_index("section") == ends[pipe]
            result = jnp.where(at_end, loss_ref[tick], result)
        y_ref[...] = result


def layer_back(parts, up, down, tick, ends):
    like = jax.ShapeDtypeStruct(up[1].shape, jnp.bfloat16)
    return local_call(
        functools.partial(layer_back_body, tick, ends),
        [like, like],
        (parts, *up, *down),
        flops=20 * parts.size,
        moved=3 * parts.size,
    )


def qkv_gradient_body(start, later, mirrored, *rest):
    factors, (w_ref, d_all) = rest[:6], rest[6:]
    rows = factors[0].shape[1]
    tile = start.shape[-1]

    @pl.when(pl.program_id(0) == 0)
    def _():
        for index, factor in enumerate(factors):
            for part in range(3):
                d_all[part, index * rows : (index + 1) * rows, :] = factor[part]

    def flat(block):
        return block.reshape(rows, tile)

    hidden = jnp.concatenate(
        [flat(start[:, 0]), flat(later[:, 0]), flat(later[:, 1])]
        + [flat(mirrored[:, index]) for index in range(TICKS)],
        axis=0,
    )
    turned = hidden.T
    for part in range(3):
        w_ref[part] = dot_nn(turned, d_all[part]).astype(jnp.bfloat16)


def qkv_gradient(start, later, mirrored, factors):
    shards, _, shard_rows, features = start.shape
    rows, local = factors[0].shape[1:]
    tile = 256

    def columns(count, at=0):
        return pl.BlockSpec((shards, count, shard_rows, tile), lambda i: (0, at, 0, i))

    whole = pl.BlockSpec((3, rows, local), lambda i: (0, 0, 0))
    depth = 2 * TICKS * rows
    return pl.pallas_call(
        qkv_gradient_body,
        grid=(features // tile,),
        out_shape=jax.ShapeDtypeStruct((3, features, local), jnp.bfloat16),
        in_specs=[columns(1, 2), columns(2), columns(TICKS)] + [whole] * 6,
        out_specs=pl.BlockSpec((3, tile, local), lambda i: (0, i, 0)),
        scratch_shapes=[pltpu.VMEM((3, depth, local), jnp.bfloat16)],
        compiler_params=pltpu.CompilerParams(vmem_limit_bytes=ROOM),
        cost_estimate=pl.CostEstimate(
            flops=600 * depth * features * local, bytes_accessed=800 * MIB, transcendentals=0
        ),
    )(start, later, mirrored, *factors)


def out_gradient_body(picks, *refs):
    flows, factors = refs[: len(picks)], refs[len(picks) : 2 * len(picks)]
    out_hbm, g_all, a_all, result, sem, out_sem = refs[2 * len(picks) :]
    copy = pltpu.make_async_copy
    copies = []
    for index, pick in enumerate(picks):
        copies.append(copy(factors[index].at[3], a_all.at[index], sem.at[0, index]))
        copies.append(copy(flows[index].at[:, pick], g_all.at[index], sem.at[1, index]))
    for one in copies:
        one.start()
    for one in copies:
        one.wait()
    rows, local = a_all.shape[1:]
    features = g_all.shape[-1]
    turned = a_all[...].reshape(len(picks) * rows, local).T
    tile = features // 2
    sent = []
    for index in range(2):
        cols = slice(index * tile, (index + 1) * tile)
        upstream = g_all[:, :, :, cols].reshape(len(picks) * rows, tile)
        result[:, cols] = dot_nn(turned, upstream).astype(jnp.bfloat16)
        sent.append(copy(result.at[:, cols], out_hbm.at[:, cols], out_sem.at[index]))
        sent[-1].start()
    for one in sent:
        one.wait()


def out_gradient(flows, picks, factors):
    shards, _, shard_rows, features = flows[0].shape
    rows, local = factors[0].shape[1:]
    count = len(picks)
    return local_call(
        functools.partial(out_gradient_body, picks),
        jax.ShapeDtypeStruct((local, features), jnp.bfloat16),
        (*flows, *factors),
        flops=2 * count * rows * features * local,
        moved=5 * MIB,
        in_specs=[ANY] * (2 * count),
        out_specs=ANY,
        scratch=[
            pltpu.VMEM((count, shards, shard_rows, features), jnp.bfloat16),
            pltpu.VMEM((count, rows, local), jnp.bfloat16),
            pltpu.VMEM((local, features), jnp.bfloat16),
            pltpu.SemaphoreType.DMA((2, count)),
            pltpu.SemaphoreType.DMA((2,)),
        ],
    )


def after(value, *others):
    return lax.optimization_barrier((value,) + others)[0]


def exchanged(parts):
    return lax.all_to_all(parts, "tp", split_axis=0, concat_axis=0, tiled=True)


def gathered_rows(rows):
    return lax.all_gather(rows, "tp", axis=0, tiled=False)


def per_device(
    query_key_value_weight,
    output_weight,
    ascending_query_key_value_weight,
    ascending_output_weight,
    descending_saved_input,
    ascending_saved_input,
    descending_transit_gradient,
    ascending_transit_gradient,
    descending_loss_gradient,
    ascending_loss_gradient,
):
    sections = lax.axis_size("section")
    last = sections - 1
    w_down = jnp.transpose(query_key_value_weight[0], (1, 0, 2))
    w_up = jnp.transpose(ascending_query_key_value_weight[0], (1, 0, 2))
    o_down = output_weight[0]
    o_up = ascending_output_weight[0]
    x_down = descending_saved_input[0]
    x_up = ascending_saved_input[0]
    flow_down = descending_transit_gradient[0]
    flow_up = ascending_transit_gradient[0]

    lower = [(index, (index - 1) % sections) for index in range(sections)]
    upper = [(index, (index + 1) % sections) for index in range(sections)]
    across = [(index, last - index) for index in range(sections)]

    start, h_later, sent = prepare(x_down, x_up, flow_down, flow_up)
    start = exchanged(start)
    start, h_later, sent = lax.optimization_barrier((start, h_later, sent))
    later = gathered_rows(h_later)
    sent = lax.ppermute(sent, "section", across)

    saved = forward(start, ((0,), (2,)), w_up, w_down)
    gathered, picks = start, (1, 3)
    flows, added, factors, mirrored_factors = [], [], [], []
    for tick in range(TICKS):
        final = tick + 1 == TICKS
        parts, factor_up, factor_down = backward(
            gathered, picks, saved[tick], w_up, w_down, o_up, o_down, added
        )
        factors.append(factor_down)
        if tick == 0:
            parts, sent = lax.optimization_barrier((parts, sent))
        else:
            parts, mirrored_factors[-1] = lax.optimization_barrier((parts, mirrored_factors[-1]))
        if tick == 1:
            parts, row_up = lax.optimization_barrier((parts, row_up))
            mirrored = gathered_rows(jnp.concatenate([sent, row_up[None]], axis=0))
        parts = exchanged(parts)
        if final:
            mirrored_factors.append(lax.ppermute(factor_up, "section", across))
            grad_qkv = qkv_gradient(start, later, mirrored, factors + mirrored_factors)
            parts, grad_qkv = lax.optimization_barrier((parts, grad_qkv))
        y_up, y_down = layer_back(
            parts,
            (x_up, flow_up, ascending_loss_gradient),
            (x_down, flow_down, descending_loss_gradient),
            tick,
            None if final else (last, 0),
        )
        if not final:
            flow_up = lax.ppermute(y_up, "section", upper)
            flow_down = lax.ppermute(y_down, "section", lower)
            gathered = repeat(flow_up, flow_down)
            gathered, row_up = lax.optimization_barrier((gathered, flow_up))
            gathered = exchanged(gathered)
            picks = (0, 1)
            flows.append(gathered)
            row_up = lax.ppermute(row_up, "section", across)
            if tick == 0:
                saved += forward(later, ((2, 3), (0, 1)), w_up, w_down)
                gathered, row_up, factor_up, saved[1:] = lax.optimization_barrier(
                    (gathered, row_up, factor_up, saved[1:])
                )
            else:
                gathered, factor_up, row_up = lax.optimization_barrier((gathered, factor_up, row_up))
                added = [row_up]
            mirrored_factors.append(lax.ppermute(factor_up, "section", across))
    grad_out = out_gradient(
        (start, *flows, mirrored, mirrored, parts),
        (3, 1, 1, TICKS, TICKS + 1, 2),
        factors + mirrored_factors,
    )
    return (
        jnp.transpose(grad_qkv, (1, 0, 2))[None],
        grad_out[None],
        y_down[None],
        y_up[None],
    )


def solution(mesh):
    in_specs = (
        P("section", None, None, "tp"),
        P("section", "tp", None),
        P("section", None, None, "tp"),
        P("section", "tp", None),
        P("section", None, "tp", None),
        P("section", None, "tp", None),
        P("section", "tp", None),
        P("section", "tp", None),
        P(None, "tp", None),
        P(None, "tp", None),
    )
    out_specs = (
        P("section", None, None, "tp"),
        P("section", "tp", None),
        P("section", "tp", None),
        P("section", "tp", None),
    )
    return jax.shard_map(
        per_device, mesh=mesh, in_specs=in_specs, out_specs=out_specs, check_vma=False
    )
```
